32 devices in a mesh: leaf: 8 (over z, y), panel: 4 (over x, core).
Axes of the slice: x: 2, y: 2, z: 4, core: 2. Of those that a mesh axis runs over, the one named last changes fastest.
Arguments:
- right_sides: float32 [7, 4096, 512], P(None, 'leaf', 'panel'), may hold values from -11 to 11
- inverse_diagonal: bfloat16 [7, 4096, 4096], P(None, 'leaf'), may hold values from -1 to 2, as said below
- off_diagonal: bfloat16 [6, 4096, 4096], P(None, 'leaf'), may hold values from -0.0625 to 0.0625
- structure: int32 [6, 32], replicated, may hold values from 0 to 95, as said below
- pivot_counts: int32 [7], replicated, may hold values from 2048 to 4096, as said below
Outputs:
- samples: float32 [7, 4096, 512], P(None, 'leaf', 'panel')
- sample_power: float32 [7, 4096], P(None, 'leaf')
The draws below stay inside these ranges and needn't reach their ends.
Inputs may be any that keep to these rules, and one draw needn't show every extreme that they name: `inverse_diagonal`: zero below the diagonal; diagonal entries positive. `structure`: a front of the middle level lists 4096 // 128 distinct blocks of the root (numbers below 32); a bottom front lists distinct blocks of the root and of its parent (parent p = 1 + (f - 3) // 2 holds block numbers p * 32 to (p + 1) * 32 - 1). `pivot_counts`: rows from the count on are padding; some front has exactly 4096 live rows and some exactly 2048.
All inputs are finite; a program needn't handle non-finite values.
Results may differ from the reference program's by a relative error of at most 0.0038.
Values may be sent and summed in bfloat16 or wider, within the bound.
A program may use at most 128 MiB of HBM per device.

```python
import math
import jax
import jax.numpy as jnp
from jax import lax

S = 4096
K = 4096
BLK = 128
RHS = 512


def draw_right_sides(key, part):
    column_scale = 0.5 + jnp.arange(RHS, dtype=jnp.float32) / jnp.float32(max(RHS - 1, 1))
    values = jax.random.normal(jax.random.fold_in(key, 5), (7, S, RHS), jnp.float32)
    result = jnp.clip(values, -6.0, 6.0) * column_scale[None, None, :]
    return result


def draw_inverse_diagonal(key, part):
    row_ids = jnp.arange(S, dtype=jnp.int32)[:, None]
    col_ids = jnp.arange(S, dtype=jnp.int32)[None, :]
    upper = (col_ids > row_ids)[None, :, :]
    on_diag = (col_ids == row_ids)[None, :, :]
    spread = jnp.clip(jax.random.normal(jax.random.fold_in(key, 8), (7, S, S), jnp.float32), -6.0, 6.0) * (0.5 / math.sqrt(S))
    diag_part = jax.random.uniform(jax.random.fold_in(key, 9), (7, S, S), jnp.float32, 0.5, 1.5)
    return jnp.where(on_diag, diag_part, jnp.where(upper, spread, 0.0)).astype(jnp.bfloat16)


def draw_structure(key, part):
    root_blocks = S // BLK
    list_length = K // BLK
    lists = []
    for front_index in range(1, 7):
        front_key = jax.random.fold_in(key, 100 + front_index)
        if front_index <= 2:
            chosen = jax.random.permutation(front_key, root_blocks)[:list_length]
            if front_index == 1:
                present = jnp.any(chosen == 0)
                chosen = chosen.at[0].set(jnp.where(present, chosen[0], 0))
        else:
            parent = 1 + (front_index - 3) // 2
            picks = jax.random.permutation(front_key, 2 * root_blocks)[:list_length]
            if front_index == 6:
                top_pick = 2 * root_blocks - 1
                present = jnp.any(picks == top_pick)
                picks = picks.at[0].set(jnp.where(present, picks[0], top_pick))
            chosen = jnp.where(picks < root_blocks, picks, parent * root_blocks + picks - root_blocks)
        lists.append(chosen.astype(jnp.int32))
    return jnp.stack(lists, axis=0).astype(jnp.int32)


def draw_pivot_counts(key, part):
    order = jax.random.permutation(jax.random.fold_in(key, 11), 7)
    counts = jax.random.randint(jax.random.fold_in(key, 12), (7,), S // 2, S + 1, jnp.int32)
    front_ids = jnp.arange(7, dtype=jnp.int32)
    counts = jnp.where(front_ids == order[0], S, counts)
    counts = jnp.where(front_ids == order[1], S // 2, counts)
    return counts.astype(jnp.int32)


def block_levels(key, shape, shards, least, top_value):
    def one(dim, parts):
        steps = jax.random.uniform(jax.random.fold_in(jax.random.fold_in(key, 6), dim), (parts,), jnp.float32, least / len(shards), top_value / len(shards))
        return jnp.repeat(jnp.exp(steps), shape[dim] // parts).reshape((-1,) + (1,) * (len(shape) - dim - 1))

    gain = one(*shards[0])
    for cut in shards[1:]:
        gain = gain * one(*cut)
    return gain


def centred(own_key, dims, scale, reach, split=(), kind=jnp.bfloat16):
    level = block_levels(own_key, dims, split, -0.22, 0.18) if split else 1.0
    values = jax.random.normal(own_key, dims, jnp.float32) * scale * level
    return jnp.minimum(jnp.maximum(values, -reach), reach).astype(kind)


def setup_inputs(seed: int = 0) -> dict:
    arg_keys = jax.random.split(jax.random.key(seed), 6)
    right_sides = draw_right_sides(jax.random.fold_in(arg_keys[5], 71), 0)
    inverse_diagonal = draw_inverse_diagonal(jax.random.fold_in(arg_keys[5], 71), 0)
    off_diagonal = centred(arg_keys[2], (6, S, K), (2 * K) ** -0.5, 0.0625, ((1, 8),))
    structure = draw_structure(jax.random.fold_in(arg_keys[5], 71), 0)
    pivot_counts = draw_pivot_counts(jax.random.fold_in(arg_keys[5], 71), 0)
    return dict(right_sides=right_sides, inverse_diagonal=inverse_diagonal, off_diagonal=off_diagonal, structure=structure, pivot_counts=pivot_counts)


def product(left, right):
    return jnp.dot(left.astype(jnp.float32), right.astype(jnp.float32), precision=lax.Precision.HIGHEST, preferred_element_type=jnp.float32)


def reference(right_sides, inverse_diagonal, off_diagonal, structure, pivot_counts):
    row_index = (structure[:, :, None] * BLK + jnp.arange(BLK, dtype=jnp.int32)[None, None, :]).reshape(6, K).astype(jnp.int32)
    position = jnp.arange(S, dtype=jnp.int32)
    solved = []
    stored = []
    for front_index in range(7):
        live_mask = (position < pivot_counts[front_index]).astype(jnp.float32)[:, None]
        if front_index == 0:
            update = jnp.zeros((S, RHS), jnp.float32)
        else:
            ancestors = jnp.concatenate(stored, axis=0)
            picked = jnp.take(ancestors, row_index[front_index - 1], axis=0)
            update = product(off_diagonal[front_index - 1], picked)
        reduced = (live_mask * (right_sides[front_index] - update)).astype(jnp.bfloat16)
        solved_field = live_mask * product(inverse_diagonal[front_index], reduced)
        solved.append(solved_field)
        stored.append(solved_field.astype(jnp.bfloat16))
    samples = jnp.stack(solved, axis=0)
    sample_power = jnp.sum(samples * samples, axis=2) / jnp.float32(RHS)
    return samples, sample_power
```

```python
import functools
import math

import jax
import jax.numpy as jnp
from jax import lax
from jax.experimental import pallas as pl
from jax.experimental.pallas import tpu as pltpu
from jax.sharding import PartitionSpec as P

SLOTS = 8
DOWN, UP, SIDE = 0, 1, 2
MESH = pl.DeviceIdType.MESH


def kernel(
    leaves, panels, total_columns,
    rhs, inv, off, structure, counts,
    out, power,
    red, root, anc0, anc1, mats, picked, acc, sums,
    mat_sem, send_sem, recv_sem, sums_send, sums_recv,
):
    leaf = lax.axis_index("leaf")
    panel = lax.axis_index("panel")
    depth = leaves // 2
    z, y = leaf // 2, leaf % 2
    rows, columns = rhs.shape[1], rhs.shape[2]
    pivots = red.shape[1]
    coupled = off.shape[2]
    listed = structure.shape[1]
    block = coupled // listed
    pair = 2 * rows
    wide = min(coupled, 1024)
    unit = root.shape[1]
    units, piece_units = pivots // unit, rows // unit

    sequence = [(inv, 0), (off, 0), (off, 1), (inv, 1), (inv, 2)]
    sequence += [(off, 2 + i) for i in range(4)] + [(inv, 3 + i) for i in range(4)]

    def load(i):
        source, which = sequence[i]
        slot = i % SLOTS
        return pltpu.make_async_copy(source.at[which], mats.at[slot], mat_sem.at[slot])

    def release(i):
        if i + SLOTS < len(sequence):
            load(i + SLOTS).start()

    for i in range(min(SLOTS, len(sequence))):
        load(i).start()

    has_down, has_up = z > 0, z < depth - 1

    barrier = pltpu.get_barrier_semaphore()

    def greet(target):
        pl.semaphore_signal(barrier, inc=1, device_id=target, device_id_type=MESH)

    below, above, beside = leaf - 2, leaf + 2, leaf + 1 - 2 * y
    pl.when(has_down)(lambda: greet({"leaf": below}))
    pl.when(has_up)(lambda: greet({"leaf": above}))
    greet({"leaf": beside})
    for hop in range(1, panels):
        greet({"panel": lax.rem(panel + hop, panels)})
    pl.semaphore_wait(barrier, panels + has_down.astype(jnp.int32) + has_up.astype(jnp.int32))

    def rows_of(gather, piece):
        if gather < 7:
            return red.at[gather, pl.ds(pl.multiple_of(piece * rows, rows), rows)]
        if gather == 7:
            return root.at[pl.ds(piece * piece_units, piece_units)]
        return (anc0, anc1)[gather - 8].at[pl.ds(units + piece * piece_units, piece_units)]

    def transfer(gather, layer, side, way):
        piece = 2 * layer + side
        held = rows_of(gather, piece)
        return pltpu.make_async_remote_copy(
            src_ref=held,
            dst_ref=held,
            send_sem=send_sem.at[gather, way, layer],
            recv_sem=recv_sem.at[gather, piece],
            device_id={"leaf": (below, above, beside)[way]},
            device_id_type=MESH,
        )

    def send(gather, layer, way, allowed=None):
        if allowed is None:
            transfer(gather, layer, y, way).start()
        else:
            pl.when(allowed)(lambda: transfer(gather, layer, y, way).start())

    def arrived(gather, layer, side):
        transfer(gather, layer, side, SIDE).wait_recv()

    position = leaf * rows + lax.broadcasted_iota(jnp.int32, (rows, columns), 0)

    def live(front):
        return jnp.clip(counts[front] - position, 0, 1).astype(jnp.float32)

    def publish_reduced(front, update):
        value = rhs[front] if update is None else rhs[front] - update
        rows_of(front, leaf)[...] = (live(front) * value).astype(jnp.bfloat16)
        send(front, z, DOWN, has_down)
        send(front, z, SIDE)

    def couple(front, order, ancestors):
        parts = block // unit
        for i in range(listed):
            number = structure[front - 1, i]
            if ancestors is anc1:
                per_front = pivots // block
                number = jnp.minimum(number, jnp.maximum(number - per_front, per_front - 1))
            for j in range(parts):
                picked[pl.ds(i * block + j * unit, unit), :] = ancestors[number * parts + j]
        load(order).wait()
        acc[0] = jnp.zeros((rows, columns), jnp.float32)

        @pl.loop(0, coupled // wide)
        def _(i):
            start = pl.multiple_of(i * wide, wide)
            acc[0] += jnp.dot(
                mats[order % SLOTS, :, pl.ds(start, wide)],
                picked[pl.ds(start, wide), :],
                preferred_element_type=jnp.float32,
            )

        release(order)
        publish_reduced(front, acc[0])

    def finish(front):
        solved = live(front) * acc[front % 4]
        out[front] = solved
        if front < 3:
            gather = 7 + front
            rows_of(gather, leaf)[...] = solved.astype(jnp.bfloat16).reshape(piece_units, unit, columns)
            send(gather, z, DOWN, has_down)
            send(gather, z, UP, has_up)
            send(gather, z, SIDE)
        tall = min(rows, 128)
        for i in range(rows // tall):
            part = solved[i * tall:(i + 1) * tall]
            sums[panel, pl.ds(front, 1), i * tall:(i + 1) * tall] = jnp.sum(
                (part * part).T, axis=0, keepdims=True
            )

    def solve(fronts, orders):
        for front in fronts:
            acc[front % 4] = jnp.zeros((rows, columns), jnp.float32)

        @pl.loop(1, depth - z + 1)
        def _(step):
            layer = z + step

            @pl.when(layer < depth)
            def _():
                for front in fronts:
                    arrived(front, layer, y)
                    send(front, layer, DOWN, has_down)
                    send(front, layer, SIDE)

            done = layer - 1
            start = pl.multiple_of(done * pair, pair)
            for front, order in zip(fronts, orders):
                arrived(front, done, 1 - y)
                pl.when(step == 1)(lambda: load(order).wait())
                acc[front % 4] += jnp.dot(
                    mats[order % SLOTS, :, pl.ds(start, pair)],
                    red[front, pl.ds(start, pair), :],
                    preferred_element_type=jnp.float32,
                )
                pl.when(layer == depth)(lambda: finish(front))

        for order in orders:
            release(order)

    def share(fronts):
        @pl.loop(1, depth)
        def _(step):
            for front in fronts:
                gather = 7 + front

                @pl.when(z + step < depth)
                def _():
                    arrived(gather, z + step, y)
                    send(gather, z + step, DOWN, has_down)
                    send(gather, z + step, SIDE)

                @pl.when(z - step >= 0)
                def _():
                    arrived(gather, z - step, y)
                    send(gather, z - step, UP, has_up)
                    send(gather, z - step, SIDE)

    def share_end(front):
        @pl.loop(0, depth)
        def _(layer):
            arrived(7 + front, layer, 1 - y)

    publish_reduced(0, None)
    solve([0], [0])
    share([0])
    share_end(0)
    couple(1, 1, root)
    couple(2, 2, root)
    anc0[0:units] = root[...]
    anc1[0:units] = root[...]
    solve([1, 2], [3, 4])
    share([1, 2])
    share_end(1)
    couple(3, 5, anc0)
    couple(4, 6, anc0)
    share_end(2)
    couple(5, 7, anc1)
    couple(6, 8, anc1)
    solve([3, 4, 5, 6], [9, 10, 11, 12])

    def exchange(hop):
        return pltpu.make_async_remote_copy(
            src_ref=sums.at[panel],
            dst_ref=sums.at[panel],
            send_sem=sums_send.at[hop],
            recv_sem=sums_recv.at[hop],
            device_id={"panel": lax.rem(panel + hop, panels)},
            device_id_type=MESH,
        )

    for hop in range(1, panels):
        exchange(hop).start()

    @pl.loop(z, depth)
    def _(layer):
        for front in range(7):
            pl.when(has_down)(lambda: transfer(front, layer, y, DOWN).wait_send())
            transfer(front, layer, y, SIDE).wait_send()

    @pl.loop(0, depth)
    def _(layer):
        for gather in range(7, 10):
            pl.when(has_down & (layer >= z))(lambda: transfer(gather, layer, y, DOWN).wait_send())
            pl.when(has_up & (layer <= z))(lambda: transfer(gather, layer, y, UP).wait_send())
            transfer(gather, layer, y, SIDE).wait_send()

    for hop in range(1, panels):
        exchange(hop).wait()
    total = sums[0]
    for i in range(1, panels):
        total = total + sums[i]
    power[...] = total[0:7] / jnp.float32(total_columns)


def local(leaves, panels, right_sides, inverse_diagonal, off_diagonal, structure, pivot_counts):
    fronts, rows, columns = right_sides.shape
    pivots = inverse_diagonal.shape[2]
    coupled = off_diagonal.shape[2]
    unit = math.gcd(rows, coupled // structure.shape[1])
    bf16, f32 = jnp.bfloat16, jnp.float32
    vmem = pl.BlockSpec(memory_space=pltpu.VMEM)
    smem = pl.BlockSpec(memory_space=pltpu.SMEM)
    anywhere = pl.BlockSpec(memory_space=pl.ANY)
    return pl.pallas_call(
        functools.partial(kernel, leaves, panels, columns * panels),
        out_shape=(
            jax.ShapeDtypeStruct((fronts, rows, columns), f32),
            jax.ShapeDtypeStruct((fronts, rows), f32),
        ),
        in_specs=[vmem, anywhere, anywhere, smem, smem],
        out_specs=(vmem, vmem),
        scratch_shapes=[
            pltpu.VMEM((7, pivots, columns), bf16),
            pltpu.VMEM((pivots // unit, unit, columns), bf16),
            pltpu.VMEM((2 * pivots // unit, unit, columns), bf16),
            pltpu.VMEM((2 * pivots // unit, unit, columns), bf16),
            pltpu.VMEM((SLOTS, rows, max(pivots, coupled)), bf16),
            pltpu.VMEM((coupled, columns), bf16),
            pltpu.VMEM((4, rows, columns), f32),
            pltpu.VMEM((panels, 8, rows), f32),
            pltpu.SemaphoreType.DMA((SLOTS,)),
            pltpu.SemaphoreType.DMA((10, 3, leaves // 2)),
            pltpu.SemaphoreType.DMA((10, leaves)),
            pltpu.SemaphoreType.DMA((panels,)),
            pltpu.SemaphoreType.DMA((panels,)),
        ],
        compiler_params=pltpu.CompilerParams(
            collective_id=0, has_side_effects=True, vmem_limit_bytes=58 * 2**20
        ),
        cost_estimate=pl.CostEstimate(
            flops=13 * 2 * rows * pivots * columns,
            bytes_accessed=13 * 2 * rows * pivots,
            transcendentals=0,
        ),
    )(right_sides, inverse_diagonal, off_diagonal, structure, pivot_counts)


def solution(mesh):
    placed = (P(None, "leaf", "panel"), P(None, "leaf", None), P(None, "leaf", None), P(), P())
    return jax.shard_map(
        functools.partial(local, mesh.shape["leaf"], mesh.shape["panel"]),
        mesh=mesh,
        in_specs=placed,
        out_specs=(P(None, "leaf", "panel"), P(None, "leaf")),
        check_vma=False,
    )
```

```python
import functools
import math

import jax
import jax.numpy as jnp
from jax import lax
from jax.experimental import pallas as pl
from jax.experimental.pallas import tpu as pltpu
from jax.sharding import PartitionSpec as P

SLOTS = 8
CHUNKS = 2
CROSSING = 1
DOWN, UP, SIDE = 0, 1, 2
MESH = pl.DeviceIdType.MESH


def kernel(
    leaves, panels, total_columns,
    rhs, inv, off, structure, counts,
    out, power,
    red, root, anc0, anc1, mats, picked, acc, sums,
    mat_sem, send_sem, cross_sem, recv_sem, sums_send, sums_recv,
):
    leaf = lax.axis_index("leaf")
    panel = lax.axis_index("panel")
    depth = leaves // 2
    z, y = leaf // 2, leaf % 2
    rows, columns = rhs.shape[1], rhs.shape[2]
    pivots = red.shape[1]
    coupled = off.shape[2]
    listed = structure.shape[1]
    block = coupled // listed
    pair = 2 * rows
    wide = min(coupled, 1024)
    unit = root.shape[1]
    units, piece_units = pivots // unit, rows // unit

    sequence = [(inv, 0), (off, 0), (off, 1), (inv, 1), (inv, 2)]
    sequence += [(off, 2 + i) for i in range(4)] + [(inv, 3 + i) for i in range(4)]

    def load(i):
        source, which = sequence[i]
        slot = i % SLOTS
        return pltpu.make_async_copy(source.at[which], mats.at[slot], mat_sem.at[slot])

    def release(i):
        if i + SLOTS < len(sequence):
            load(i + SLOTS).start()

    for i in range(min(SLOTS, len(sequence))):
        load(i).start()

    has_down, has_up = z > 0, z < depth - 1

    barrier = pltpu.get_barrier_semaphore()

    def greet(target):
        pl.semaphore_signal(barrier, inc=1, device_id=target, device_id_type=MESH)

    below, above, beside = leaf - 2, leaf + 2, leaf + 1 - 2 * y
    pl.when(has_down)(lambda: greet({"leaf": below}))
    pl.when(has_up)(lambda: greet({"leaf": above}))
    greet({"leaf": beside})
    for hop in range(1, panels):
        greet({"panel": lax.rem(panel + hop, panels)})
    pl.semaphore_wait(barrier, panels + has_down.astype(jnp.int32) + has_up.astype(jnp.int32))

    def rows_of(gather, piece, chunk, chunks=CHUNKS):
        index = piece * chunks + chunk
        if gather < 7:
            size = rows // chunks
            return red.at[gather, pl.ds(pl.multiple_of(index * size, size), size)]
        size = piece_units // chunks
        if gather == 7:
            return root.at[pl.ds(index * size, size)]
        return (anc0, anc1)[gather - 8].at[pl.ds(units + index * size, size)]

    def transfer(gather, layer, side, chunk, way, cross=False):
        piece = 2 * layer + side
        held = rows_of(gather, piece, chunk)
        place = layer * CHUNKS + chunk
        return pltpu.make_async_remote_copy(
            src_ref=held,
            dst_ref=held,
            send_sem=cross_sem.at[gather, way, chunk] if cross else send_sem.at[gather, way, place],
            recv_sem=recv_sem.at[gather, piece * CHUNKS + chunk],
            device_id={"leaf": (below, above, beside)[way]},
            device_id_type=MESH,
        )

    first_cross = CHUNKS - CROSSING

    def send(gather, layer, chunk, way):
        transfer(gather, layer, y, chunk, way).start()

    def arrived(gather, layer, side, chunk):
        transfer(gather, layer, side, chunk, SIDE).wait_recv()

    def relay(gather, layer, way, allowed):
        for chunk in range(CHUNKS):
            arrived(gather, layer, y, chunk)
            pl.when(allowed)(lambda: send(gather, layer, chunk, way))
            if chunk < first_cross:
                send(gather, layer, chunk, SIDE)
            else:
                near = (layer == z - 1) | (layer == z + 1)
                pl.when(jnp.logical_not(near))(lambda: send(gather, layer, chunk, SIDE))

    def cross(gather, upward):
        for chunk in range(first_cross, CHUNKS):
            arrived(gather, z, 1 - y, chunk)
            if upward:
                pl.when(has_up)(lambda: transfer(gather, z, 1 - y, chunk, UP, True).start())
            pl.when(has_down)(lambda: transfer(gather, z, 1 - y, chunk, DOWN, True).start())

    def publish(gather, upward):
        for chunk in range(CHUNKS):
            if upward:
                pl.when(has_up)(lambda: send(gather, z, chunk, UP))
            pl.when(has_down)(lambda: send(gather, z, chunk, DOWN))
            send(gather, z, chunk, SIDE)

    position = leaf * rows + lax.broadcasted_iota(jnp.int32, (rows, columns), 0)

    def live(front):
        return jnp.clip(counts[front] - position, 0, 1).astype(jnp.float32)

    def publish_reduced(front, update):
        value = rhs[front] if update is None else rhs[front] - update
        rows_of(front, leaf, 0, 1)[...] = (live(front) * value).astype(jnp.bfloat16)
        publish(front, False)

    def couple(front, order, ancestors):
        parts = block // unit
        for i in range(listed):
            number = structure[front - 1, i]
            if ancestors is anc1:
                per_front = pivots // block
                number = jnp.minimum(number, jnp.maximum(number - per_front, per_front - 1))
            for j in range(parts):
                picked[pl.ds(i * block + j * unit, unit), :] = ancestors[number * parts + j]
        load(order).wait()
        acc[0] = jnp.zeros((rows, columns), jnp.float32)

        @pl.loop(0, coupled // wide)
        def _(i):
            start = pl.multiple_of(i * wide, wide)
            acc[0] += jnp.dot(
                mats[order % SLOTS, :, pl.ds(start, wide)],
                picked[pl.ds(start, wide), :],
                preferred_element_type=jnp.float32,
            )

        release(order)
        publish_reduced(front, acc[0])

    def finish(front):
        solved = live(front) * acc[front % 4]
        out[front] = solved
        if front < 3:
            gather = 7 + front
            rows_of(gather, leaf, 0, 1)[...] = solved.astype(jnp.bfloat16).reshape(piece_units, unit, columns)
            publish(gather, True)
        tall = min(rows, 128)
        for i in range(rows // tall):
            part = solved[i * tall:(i + 1) * tall]
            sums[panel, pl.ds(front, 1), i * tall:(i + 1) * tall] = jnp.sum(
                (part * part).T, axis=0, keepdims=True
            )

    def solve(fronts, orders):
        for front in fronts:
            acc[front % 4] = jnp.zeros((rows, columns), jnp.float32)

        @pl.loop(1, depth - z + 1)
        def _(step):
            layer = z + step

            for front in fronts:
                pl.when(layer < depth)(lambda: relay(front, layer, DOWN, has_down))
                pl.when(step == 1)(lambda: cross(front, False))

            done = layer - 1
            start = pl.multiple_of(done * pair, pair)
            for front, order in zip(fronts, orders):
                for chunk in range(first_cross):
                    arrived(front, done, 1 - y, chunk)

                @pl.when(done > z)
                def _():
                    for chunk in range(first_cross, CHUNKS):
                        arrived(front, done, 1 - y, chunk)

                pl.when(step == 1)(lambda: load(order).wait())
                acc[front % 4] += jnp.dot(
                    mats[order % SLOTS, :, pl.ds(start, pair)],
                    red[front, pl.ds(start, pair), :],
                    preferred_element_type=jnp.float32,
                )
                pl.when(layer == depth)(lambda: finish(front))

        for order in orders:
            release(order)

    def share(fronts):
        @pl.loop(z + 1, depth)
        def _(layer):
            for front in fronts:
                relay(7 + front, layer, DOWN, has_down)

        for front in fronts:
            cross(7 + front, True)

        @pl.loop(1, z + 1)
        def _(step):
            for front in fronts:
                relay(7 + front, z - step, UP, has_up)

    def share_end(front):
        @pl.loop(0, depth)
        def _(layer):
            for chunk in range(first_cross):
                arrived(7 + front, layer, 1 - y, chunk)

            @pl.when(layer != z)
            def _():
                for chunk in range(first_cross, CHUNKS):
                    arrived(7 + front, layer, 1 - y, chunk)

    publish_reduced(0, None)
    solve([0], [0])
    share([0])
    share_end(0)
    couple(1, 1, root)
    couple(2, 2, root)
    anc0[0:units] = root[...]
    anc1[0:units] = root[...]
    solve([1, 2], [3, 4])
    share([1, 2])
    share_end(1)
    couple(3, 5, anc0)
    couple(4, 6, anc0)
    share_end(2)
    couple(5, 7, anc1)
    couple(6, 8, anc1)
    solve([3, 4, 5, 6], [9, 10, 11, 12])

    def exchange(hop):
        return pltpu.make_async_remote_copy(
            src_ref=sums.at[panel],
            dst_ref=sums.at[panel],
            send_sem=sums_send.at[hop],
            recv_sem=sums_recv.at[hop],
            device_id={"panel": lax.rem(panel + hop, panels)},
            device_id_type=MESH,
        )

    for hop in range(1, panels):
        exchange(hop).start()

    def left(gather, layer, chunk, way, allowed=None):
        if allowed is None:
            transfer(gather, layer, y, chunk, way).wait_send()
        else:
            pl.when(allowed)(lambda: transfer(gather, layer, y, chunk, way).wait_send())

    @pl.loop(0, depth)
    def _(layer):
        near = (layer == z - 1) | (layer == z + 1)
        for gather in range(10):
            for chunk in range(CHUNKS):
                sideways = layer >= 0 if gather >= 7 else layer >= z
                if chunk >= first_cross:
                    sideways = sideways & jnp.logical_not(near)
                left(gather, layer, chunk, SIDE, sideways)
                left(gather, layer, chunk, DOWN, has_down & (layer >= z))
                if gather >= 7:
                    left(gather, layer, chunk, UP, has_up & (layer <= z))

    for gather in range(10):
        for chunk in range(first_cross, CHUNKS):
            pl.when(has_down)(lambda: transfer(gather, z, 1 - y, chunk, DOWN, True).wait_send())
            if gather >= 7:
                pl.when(has_up)(lambda: transfer(gather, z, 1 - y, chunk, UP, True).wait_send())

    for hop in range(1, panels):
        exchange(hop).wait()
    total = sums[0]
    for i in range(1, panels):
        total = total + sums[i]
    power[...] = total[0:7] / jnp.float32(total_columns)


def local(leaves, panels, right_sides, inverse_diagonal, off_diagonal, structure, pivot_counts):
    fronts, rows, columns = right_sides.shape
    pivots = inverse_diagonal.shape[2]
    coupled = off_diagonal.shape[2]
    unit = math.gcd(rows // CHUNKS, coupled // structure.shape[1])
    bf16, f32 = jnp.bfloat16, jnp.float32
    vmem = pl.BlockSpec(memory_space=pltpu.VMEM)
    smem = pl.BlockSpec(memory_space=pltpu.SMEM)
    anywhere = pl.BlockSpec(memory_space=pl.ANY)
    return pl.pallas_call(
        functools.partial(kernel, leaves, panels, columns * panels),
        out_shape=(
            jax.ShapeDtypeStruct((fronts, rows, columns), f32),
            jax.ShapeDtypeStruct((fronts, rows), f32),
        ),
        in_specs=[vmem, anywhere, anywhere, smem, smem],
        out_specs=(vmem, vmem),
        scratch_shapes=[
            pltpu.VMEM((7, pivots, columns), bf16),
            pltpu.VMEM((pivots // unit, unit, columns), bf16),
            pltpu.VMEM((2 * pivots // unit, unit, columns), bf16),
            pltpu.VMEM((2 * pivots // unit, unit, columns), bf16),
            pltpu.VMEM((SLOTS, rows, max(pivots, coupled)), bf16),
            pltpu.VMEM((coupled, columns), bf16),
            pltpu.VMEM((4, rows, columns), f32),
            pltpu.VMEM((panels, 8, rows), f32),
            pltpu.SemaphoreType.DMA((SLOTS,)),
            pltpu.SemaphoreType.DMA((10, 3, CHUNKS * leaves // 2)),
            pltpu.SemaphoreType.DMA((10, 2, CHUNKS)),
            pltpu.SemaphoreType.DMA((10, CHUNKS * leaves)),
            pltpu.SemaphoreType.DMA((panels,)),
            pltpu.SemaphoreType.DMA((panels,)),
        ],
        compiler_params=pltpu.CompilerParams(
            collective_id=0, has_side_effects=True, vmem_limit_bytes=58 * 2**20
        ),
        cost_estimate=pl.CostEstimate(
            flops=13 * 2 * rows * pivots * columns,
            bytes_accessed=13 * 2 * rows * pivots,
            transcendentals=0,
        ),
    )(right_sides, inverse_diagonal, off_diagonal, structure, pivot_counts)


def solution(mesh):
    placed = (P(None, "leaf", "panel"), P(None, "leaf", None), P(None, "leaf", None), P(), P())
    return jax.shard_map(
        functools.partial(local, mesh.shape["leaf"], mesh.shape["panel"]),
        mesh=mesh,
        in_specs=placed,
        out_specs=(P(None, "leaf", "panel"), P(None, "leaf")),
        check_vma=False,
    )
```

```python
import functools
import math

import jax
import jax.numpy as jnp
from jax import lax
from jax.experimental import pallas as pl
from jax.experimental.pallas import tpu as pltpu
from jax.sharding import PartitionSpec as P

SLOTS = 7
HELPED = (3, 4)
DOWN, UP, SIDE = 0, 1, 2
MESH = pl.DeviceIdType.MESH


def share_chunks(rows):
    return max(2, min(4, rows // 32))


def kernel(
    leaves, panels, total_columns,
    rhs, inv, off, structure, counts,
    out, power,
    red, root, anc0, anc1, mats, picked, acc, sums, lent, helping, part,
    mat_sem, send_sem, cross_sem, recv_sem, sums_send, sums_recv,
    lend_send, lend_recv, share_send, part_send, part_recv,
):
    leaf = lax.axis_index("leaf")
    panel = lax.axis_index("panel")
    depth = leaves // 2
    z, y = leaf // 2, leaf % 2
    rows, columns = rhs.shape[1], rhs.shape[2]
    pivots = red.shape[1]
    coupled = off.shape[2]
    listed = structure.shape[1]
    block = coupled // listed
    pair = 2 * rows
    wide = min(coupled, 1024)
    unit = root.shape[1]

    def chunks_of(gather):
        return 2 if gather < 7 else share_chunks(rows)

    units, piece_units = pivots // unit, rows // unit

    sequence = [(inv, 0), (off, 0), (off, 1), (inv, 1), (inv, 2)]
    sequence += [(off, 2 + i) for i in range(4)] + [(inv, 3 + i) for i in range(4)]

    def load(i):
        source, which = sequence[i]
        slot = i % SLOTS
        return pltpu.make_async_copy(source.at[which], mats.at[slot], mat_sem.at[slot])

    def release(i):
        if i + SLOTS < len(sequence):
            load(i + SLOTS).start()

    for i in range(min(SLOTS, len(sequence))):
        load(i).start()

    has_down, has_up = z > 0, z < depth - 1

    barrier = pltpu.get_barrier_semaphore()

    def greet(target):
        pl.semaphore_signal(barrier, inc=1, device_id=target, device_id_type=MESH)

    below, above, beside = leaf - 2, leaf + 2, leaf + 1 - 2 * y
    pl.when(has_down)(lambda: greet({"leaf": below}))
    pl.when(has_up)(lambda: greet({"leaf": above}))
    greet({"leaf": beside})
    for hop in range(1, panels):
        greet({"panel": lax.rem(panel + hop, panels)})
    pl.semaphore_wait(barrier, panels + has_down.astype(jnp.int32) + has_up.astype(jnp.int32))

    def rows_of(gather, piece, chunk, chunks):
        index = piece * chunks + chunk
        if gather < 7:
            size = rows // chunks
            return red.at[gather, pl.ds(pl.multiple_of(index * size, size), size)]
        size = piece_units // chunks
        if gather == 7:
            return root.at[pl.ds(index * size, size)]
        return (anc0, anc1)[gather - 8].at[pl.ds(units + index * size, size)]

    def transfer(gather, layer, side, chunk, way, cross=False):
        piece = 2 * layer + side
        chunks = chunks_of(gather)
        held = rows_of(gather, piece, chunk, chunks)
        place = layer * chunks + chunk
        return pltpu.make_async_remote_copy(
            src_ref=held,
            dst_ref=held,
            send_sem=cross_sem.at[gather, way, chunk] if cross else send_sem.at[gather, way, place],
            recv_sem=recv_sem.at[gather, piece * chunks + chunk],
            device_id={"leaf": (below, above, beside)[way]},
            device_id_type=MESH,
        )

    def send(gather, layer, chunk, way):
        transfer(gather, layer, y, chunk, way).start()

    def arrived(gather, layer, side, chunk):
        transfer(gather, layer, side, chunk, SIDE).wait_recv()

    def sinks(gather):
        return z > 1 if gather in HELPED else has_down

    def relay(gather, layer, way):
        for chunk in range(chunks_of(gather)):
            arrived(gather, layer, y, chunk)
            pl.when(has_up if way == UP else sinks(gather))(lambda: send(gather, layer, chunk, way))
            if chunk < chunks_of(gather) // 2:
                send(gather, layer, chunk, SIDE)
            else:
                near = (layer == z - 1) | (layer == z + 1)
                pl.when(jnp.logical_not(near))(lambda: send(gather, layer, chunk, SIDE))

    def cross(gather, upward):
        for chunk in range(chunks_of(gather) // 2, chunks_of(gather)):
            arrived(gather, z, 1 - y, chunk)
            if upward:
                pl.when(has_up)(lambda: transfer(gather, z, 1 - y, chunk, UP, True).start())
            pl.when(sinks(gather))(lambda: transfer(gather, z, 1 - y, chunk, DOWN, True).start())

    def publish(gather, upward):
        for chunk in range(chunks_of(gather)):
            if upward:
                pl.when(has_up)(lambda: send(gather, z, chunk, UP))
            pl.when(sinks(gather))(lambda: send(gather, z, chunk, DOWN))
            send(gather, z, chunk, SIDE)

    position = leaf * rows + lax.broadcasted_iota(jnp.int32, (rows, columns), 0)

    def live(front):
        return jnp.clip(counts[front] - position, 0, 1).astype(jnp.float32)

    def publish_reduced(front, update):
        value = rhs[front] if update is None else rhs[front] - update
        rows_of(front, leaf, 0, 1)[...] = (live(front) * value).astype(jnp.bfloat16)
        publish(front, False)

    def couple(front, order, ancestors):
        parts = block // unit
        for i in range(listed):
            number = structure[front - 1, i]
            if ancestors is anc1:
                per_front = pivots // block
                number = jnp.minimum(number, jnp.maximum(number - per_front, per_front - 1))
            for j in range(parts):
                picked[pl.ds(i * block + j * unit, unit), :] = ancestors[number * parts + j]
        load(order).wait()
        acc[0] = jnp.zeros((rows, columns), jnp.float32)

        @pl.loop(0, coupled // wide)
        def _(i):
            start = pl.multiple_of(i * wide, wide)
            acc[0] += jnp.dot(
                mats[order % SLOTS, :, pl.ds(start, wide)],
                picked[pl.ds(start, wide), :],
                preferred_element_type=jnp.float32,
            )

        release(order)
        publish_reduced(front, acc[0])

    share_rows = rows // panels

    def lent_rows(i, quarter):
        return lent.at[i, pl.ds(pl.multiple_of(quarter * share_rows, share_rows), share_rows)]

    def lend(i):
        taken = pl.ds(pl.multiple_of(panel * share_rows, share_rows), share_rows)
        return pltpu.make_async_remote_copy(
            src_ref=inv.at[HELPED[i], taken, pl.ds(pair, pivots - pair)],
            dst_ref=lent_rows(i, panel),
            send_sem=lend_send.at[i],
            recv_sem=lend_recv.at[i, 0],
            device_id={"leaf": above},
            device_id_type=MESH,
        )

    def pass_on(i, hop):
        return pltpu.make_async_remote_copy(
            src_ref=lent_rows(i, panel),
            dst_ref=lent_rows(i, panel),
            send_sem=share_send.at[i, hop],
            recv_sem=lend_recv.at[i, hop],
            device_id={"panel": lax.rem(panel + hop, panels)},
            device_id_type=MESH,
        )

    def lend_out(i):
        pl.when(z == 0)(lambda: lend(i).start())

    def pass_around(i):
        @pl.when(z == 1)
        def _():
            lend(i).wait_recv()
            for hop in range(1, panels):
                pass_on(i, hop).start()

    def lent_here(i):
        @pl.when(z == 1)
        def _():
            for hop in range(1, panels):
                pass_on(i, hop).wait()
            helping[i] = jnp.zeros((rows, columns), jnp.float32)

        pl.when(z == 0)(lambda: lend(i).wait_send())

    def hand(i):
        return pltpu.make_async_remote_copy(
            src_ref=part.at[i],
            dst_ref=part.at[i],
            send_sem=part_send.at[i],
            recv_sem=part_recv.at[i],
            device_id={"leaf": below},
            device_id_type=MESH,
        )

    def finish(front):
        if front in HELPED:
            i = HELPED.index(front)

            @pl.when(z == 0)
            def _():
                hand(i).wait_recv()
                acc[front % 4] += part[i].astype(jnp.float32)

        solved = live(front) * acc[front % 4]
        out[front] = solved
        if front < 3:
            gather = 7 + front
            rows_of(gather, leaf, 0, 1)[...] = solved.astype(jnp.bfloat16).reshape(piece_units, unit, columns)
            publish(gather, True)
        tall = min(rows, 128)
        for i in range(rows // tall):
            strip = solved[i * tall:(i + 1) * tall]
            sums[panel, pl.ds(front, 1), i * tall:(i + 1) * tall] = jnp.sum(
                (strip * strip).T, axis=0, keepdims=True
            )

    def solve(fronts, orders):
        for front in fronts:
            acc[front % 4] = jnp.zeros((rows, columns), jnp.float32)

        @pl.loop(1, depth - z + 1)
        def _(step):
            layer = z + step

            for front in fronts:
                more = layer < depth
                if front in HELPED:
                    more = more & (z > 0)
                pl.when(more)(lambda: relay(front, layer, DOWN))
                pl.when(step == 1)(lambda: cross(front, False))

            done = layer - 1
            start = pl.multiple_of(done * pair, pair)
            def gain(front, order):
                for chunk in range(chunks_of(front) // 2):
                    arrived(front, done, 1 - y, chunk)

                @pl.when(done > z)
                def _():
                    for chunk in range(chunks_of(front) // 2, chunks_of(front)):
                        arrived(front, done, 1 - y, chunk)

                pl.when(step == 1)(lambda: load(order).wait())
                acc[front % 4] += jnp.dot(
                    mats[order % SLOTS, :, pl.ds(start, pair)],
                    red[front, pl.ds(start, pair), :],
                    preferred_element_type=jnp.float32,
                )

            def help_below(front):
                i = HELPED.index(front)
                helping[i] += jnp.dot(
                    lent[i, :, pl.ds(pl.multiple_of(start - pair, pair), pair)],
                    red[front, pl.ds(start, pair), :],
                    preferred_element_type=jnp.float32,
                )

                @pl.when(layer == depth)
                def _():
                    part[i] = helping[i].astype(jnp.bfloat16)
                    hand(i).start()

            for front, order in zip(fronts, orders):
                if front in HELPED:
                    pl.when((z > 0) | (done == 0))(lambda: gain(front, order))
                    pl.when(z == 1)(lambda: help_below(front))
                else:
                    gain(front, order)
                pl.when(layer == depth)(lambda: finish(front))

        for order in orders:
            release(order)

    def share(fronts):
        @pl.loop(z + 1, depth)
        def _(layer):
            for front in fronts:
                relay(7 + front, layer, DOWN)

        for front in fronts:
            cross(7 + front, True)

        @pl.loop(1, z + 1)
        def _(step):
            for front in fronts:
                relay(7 + front, z - step, UP)

    def share_end(front):
        @pl.loop(0, depth)
        def _(layer):
            for chunk in range(chunks_of(7 + front) // 2):
                arrived(7 + front, layer, 1 - y, chunk)

            @pl.when(layer != z)
            def _():
                for chunk in range(chunks_of(7 + front) // 2, chunks_of(7 + front)):
                    arrived(7 + front, layer, 1 - y, chunk)

    lend_out(0)
    publish_reduced(0, None)
    solve([0], [0])
    share([0])
    share_end(0)
    lend_out(1)
    pass_around(0)
    couple(1, 1, root)
    couple(2, 2, root)
    anc0[0:units] = root[...]
    anc1[0:units] = root[...]
    solve([1, 2], [3, 4])
    pass_around(1)
    share([1, 2])
    share_end(1)
    couple(3, 5, anc0)
    couple(4, 6, anc0)
    share_end(2)
    couple(5, 7, anc1)
    couple(6, 8, anc1)
    lent_here(0)
    lent_here(1)
    solve([3, 4, 5, 6], [9, 10, 11, 12])

    def exchange(hop):
        return pltpu.make_async_remote_copy(
            src_ref=sums.at[panel],
            dst_ref=sums.at[panel],
            send_sem=sums_send.at[hop],
            recv_sem=sums_recv.at[hop],
            device_id={"panel": lax.rem(panel + hop, panels)},
            device_id_type=MESH,
        )

    for hop in range(1, panels):
        exchange(hop).start()

    def left(gather, layer, chunk, way, allowed=None):
        if allowed is None:
            transfer(gather, layer, y, chunk, way).wait_send()
        else:
            pl.when(allowed)(lambda: transfer(gather, layer, y, chunk, way).wait_send())

    @pl.loop(0, depth)
    def _(layer):
        near = (layer == z - 1) | (layer == z + 1)
        for gather in range(10):
            for chunk in range(chunks_of(gather)):
                sideways = layer >= 0 if gather >= 7 else layer >= z
                if gather in HELPED:
                    sideways = sideways & ((z > 0) | (layer == 0))
                if chunk >= chunks_of(gather) // 2:
                    sideways = sideways & jnp.logical_not(near)
                left(gather, layer, chunk, SIDE, sideways)
                left(gather, layer, chunk, DOWN, sinks(gather) & (layer >= z))
                if gather >= 7:
                    left(gather, layer, chunk, UP, has_up & (layer <= z))

    for gather in range(10):
        for chunk in range(chunks_of(gather) // 2, chunks_of(gather)):
            pl.when(sinks(gather))(lambda: transfer(gather, z, 1 - y, chunk, DOWN, True).wait_send())
            if gather >= 7:
                pl.when(has_up)(lambda: transfer(gather, z, 1 - y, chunk, UP, True).wait_send())

    for i in range(len(HELPED)):
        pl.when(z == 1)(lambda: hand(i).wait_send())

    for hop in range(1, panels):
        exchange(hop).wait()
    total = sums[0]
    for i in range(1, panels):
        total = total + sums[i]
    power[...] = total[0:7] / jnp.float32(total_columns)


def local(leaves, panels, right_sides, inverse_diagonal, off_diagonal, structure, pivot_counts):
    fronts, rows, columns = right_sides.shape
    pivots = inverse_diagonal.shape[2]
    coupled = off_diagonal.shape[2]
    unit = math.gcd(rows // share_chunks(rows), coupled // structure.shape[1])
    bf16, f32 = jnp.bfloat16, jnp.float32
    vmem = pl.BlockSpec(memory_space=pltpu.VMEM)
    smem = pl.BlockSpec(memory_space=pltpu.SMEM)
    anywhere = pl.BlockSpec(memory_space=pl.ANY)
    return pl.pallas_call(
        functools.partial(kernel, leaves, panels, columns * panels),
        out_shape=(
            jax.ShapeDtypeStruct((fronts, rows, columns), f32),
            jax.ShapeDtypeStruct((fronts, rows), f32),
        ),
        in_specs=[vmem, anywhere, anywhere, smem, smem],
        out_specs=(vmem, vmem),
        scratch_shapes=[
            pltpu.VMEM((7, pivots, columns), bf16),
            pltpu.VMEM((pivots // unit, unit, columns), bf16),
            pltpu.VMEM((2 * pivots // unit, unit, columns), bf16),
            pltpu.VMEM((2 * pivots // unit, unit, columns), bf16),
            pltpu.VMEM((SLOTS, rows, max(pivots, coupled)), bf16),
            pltpu.VMEM((coupled, columns), bf16),
            pltpu.VMEM((4, rows, columns), f32),
            pltpu.VMEM((panels, 8, rows), f32),
            pltpu.VMEM((len(HELPED), rows, pivots - 2 * rows), bf16),
            pltpu.VMEM((len(HELPED), rows, columns), f32),
            pltpu.VMEM((len(HELPED), rows, columns), bf16),
            pltpu.SemaphoreType.DMA((SLOTS,)),
            pltpu.SemaphoreType.DMA((10, 3, share_chunks(rows) * leaves // 2)),
            pltpu.SemaphoreType.DMA((10, 2, share_chunks(rows))),
            pltpu.SemaphoreType.DMA((10, share_chunks(rows) * leaves)),
            pltpu.SemaphoreType.DMA((panels,)),
            pltpu.SemaphoreType.DMA((panels,)),
            pltpu.SemaphoreType.DMA((len(HELPED),)),
            pltpu.SemaphoreType.DMA((len(HELPED), panels)),
            pltpu.SemaphoreType.DMA((len(HELPED), panels)),
            pltpu.SemaphoreType.DMA((len(HELPED),)),
            pltpu.SemaphoreType.DMA((len(HELPED),)),
        ],
        compiler_params=pltpu.CompilerParams(
            collective_id=0, has_side_effects=True, vmem_limit_bytes=60 * 2**20
        ),
        cost_estimate=pl.CostEstimate(
            flops=13 * 2 * rows * pivots * columns,
            bytes_accessed=13 * 2 * rows * pivots,
            transcendentals=0,
        ),
    )(right_sides, inverse_diagonal, off_diagonal, structure, pivot_counts)


def solution(mesh):
    placed = (P(None, "leaf", "panel"), P(None, "leaf", None), P(None, "leaf", None), P(), P())
    return jax.shard_map(
        functools.partial(local, mesh.shape["leaf"], mesh.shape["panel"]),
        mesh=mesh,
        in_specs=placed,
        out_specs=(P(None, "leaf", "panel"), P(None, "leaf")),
        check_vma=False,
    )
```

```python
import functools
import math

import jax
import jax.numpy as jnp
from jax import lax
from jax.experimental import pallas as pl
from jax.experimental.pallas import tpu as pltpu
from jax.sharding import PartitionSpec as P

SLOTS = 7
HELPED = (3, 4)
DOWN, UP, SIDE = 0, 1, 2
MESH = pl.DeviceIdType.MESH


def share_chunks(rows):
    return max(2, min(2, rows // 32))


def kernel(
    leaves, panels, total_columns,
    rhs, inv, off, structure, counts,
    out, power,
    red, root, anc0, anc1, mats, picked, acc, sums, lent, helping, part,
    mat_sem, send_sem, cross_sem, recv_sem, sums_send, sums_recv,
    lend_send, lend_recv, share_send, part_send, part_recv,
):
    leaf = lax.axis_index("leaf")
    panel = lax.axis_index("panel")
    depth = leaves // 2
    z, y = leaf // 2, leaf % 2
    rows, columns = rhs.shape[1], rhs.shape[2]
    pivots = red.shape[1]
    coupled = off.shape[2]
    listed = structure.shape[1]
    block = coupled // listed
    pair = 2 * rows
    wide = min(coupled, 1024)
    unit = root.shape[1]

    def chunks_of(gather):
        return 2 if gather < 7 else share_chunks(rows)

    units, piece_units = pivots // unit, rows // unit

    sequence = [(inv, 0), (off, 0), (off, 1), (inv, 1), (inv, 2)]
    sequence += [(off, 2 + i) for i in range(4)] + [(inv, 3 + i) for i in range(4)]

    def load(i):
        source, which = sequence[i]
        slot = i % SLOTS
        return pltpu.make_async_copy(source.at[which], mats.at[slot], mat_sem.at[slot])

    def release(i):
        if i + SLOTS < len(sequence):
            load(i + SLOTS).start()

    for i in range(min(SLOTS, len(sequence))):
        load(i).start()

    has_down, has_up = z > 0, z < depth - 1

    barrier = pltpu.get_barrier_semaphore()

    def greet(target):
        pl.semaphore_signal(barrier, inc=1, device_id=target, device_id_type=MESH)

    below, above, beside = leaf - 2, leaf + 2, leaf + 1 - 2 * y
    pl.when(has_down)(lambda: greet({"leaf": below}))
    pl.when(has_up)(lambda: greet({"leaf": above}))
    greet({"leaf": beside})
    for hop in range(1, panels):
        greet({"panel": lax.rem(panel + hop, panels)})
    pl.semaphore_wait(barrier, panels + has_down.astype(jnp.int32) + has_up.astype(jnp.int32))

    def rows_of(gather, piece, chunk, chunks):
        index = piece * chunks + chunk
        if gather < 7:
            size = rows // chunks
            return red.at[gather, pl.ds(pl.multiple_of(index * size, size), size)]
        size = piece_units // chunks
        if gather == 7:
            return root.at[pl.ds(index * size, size)]
        return (anc0, anc1)[gather - 8].at[pl.ds(units + index * size, size)]

    def transfer(gather, layer, side, chunk, way, cross=False):
        piece = 2 * layer + side
        chunks = chunks_of(gather)
        held = rows_of(gather, piece, chunk, chunks)
        place = layer * chunks + chunk
        return pltpu.make_async_remote_copy(
            src_ref=held,
            dst_ref=held,
            send_sem=cross_sem.at[gather, way, chunk] if cross else send_sem.at[gather, way, place],
            recv_sem=recv_sem.at[gather, piece * chunks + chunk],
            device_id={"leaf": (below, above, beside)[way]},
            device_id_type=MESH,
        )

    def send(gather, layer, chunk, way):
        transfer(gather, layer, y, chunk, way).start()

    def arrived(gather, layer, side, chunk):
        transfer(gather, layer, side, chunk, SIDE).wait_recv()

    def sinks(gather):
        return z > 1 if gather in HELPED else has_down

    def relay(gather, layer, way):
        for chunk in range(chunks_of(gather)):
            arrived(gather, layer, y, chunk)
            pl.when(has_up if way == UP else sinks(gather))(lambda: send(gather, layer, chunk, way))
            if chunk < chunks_of(gather) // 2:
                send(gather, layer, chunk, SIDE)
            else:
                near = (layer == z - 1) | (layer == z + 1)
                pl.when(jnp.logical_not(near))(lambda: send(gather, layer, chunk, SIDE))

    def cross(gather, upward):
        for chunk in range(chunks_of(gather) // 2, chunks_of(gather)):
            arrived(gather, z, 1 - y, chunk)
            if upward:
                pl.when(has_up)(lambda: transfer(gather, z, 1 - y, chunk, UP, True).start())
            pl.when(sinks(gather))(lambda: transfer(gather, z, 1 - y, chunk, DOWN, True).start())

    def publish(gather, upward):
        for chunk in range(chunks_of(gather)):
            if upward:
                pl.when(has_up)(lambda: send(gather, z, chunk, UP))
            pl.when(sinks(gather))(lambda: send(gather, z, chunk, DOWN))
            send(gather, z, chunk, SIDE)

    position = leaf * rows + lax.broadcasted_iota(jnp.int32, (rows, columns), 0)

    def live(front):
        return jnp.clip(counts[front] - position, 0, 1).astype(jnp.float32)

    def publish_reduced(front, update):
        value = rhs[front] if update is None else rhs[front] - update
        rows_of(front, leaf, 0, 1)[...] = (live(front) * value).astype(jnp.bfloat16)
        publish(front, False)

    def couple(front, order, ancestors):
        parts = block // unit
        for i in range(listed):
            number = structure[front - 1, i]
            if ancestors is anc1:
                per_front = pivots // block
                number = jnp.minimum(number, jnp.maximum(number - per_front, per_front - 1))
            for j in range(parts):
                picked[pl.ds(i * block + j * unit, unit), :] = ancestors[number * parts + j]
        load(order).wait()
        acc[0] = jnp.zeros((rows, columns), jnp.float32)

        @pl.loop(0, coupled // wide)
        def _(i):
            start = pl.multiple_of(i * wide, wide)
            acc[0] += jnp.dot(
                mats[order % SLOTS, :, pl.ds(start, wide)],
                picked[pl.ds(start, wide), :],
                preferred_element_type=jnp.float32,
            )

        release(order)
        publish_reduced(front, acc[0])

    share_rows = rows // panels

    def lent_rows(i, quarter):
        return lent.at[i, pl.ds(pl.multiple_of(quarter * share_rows, share_rows), share_rows)]

    def lend(i):
        taken = pl.ds(pl.multiple_of(panel * share_rows, share_rows), share_rows)
        return pltpu.make_async_remote_copy(
            src_ref=inv.at[HELPED[i], taken, pl.ds(pair, pivots - pair)],
            dst_ref=lent_rows(i, panel),
            send_sem=lend_send.at[i],
            recv_sem=lend_recv.at[i, 0],
            device_id={"leaf": above},
            device_id_type=MESH,
        )

    def flip(at, distance):
        return at + distance - 2 * distance * ((at // distance) % 2)

    distances = []
    while 2 ** len(distances) < panels:
        distances.append(panels // 2 ** (len(distances) + 1))

    def pass_on(i, stage, held):
        distance = distances[stage]
        quarter = panel
        for k, other in enumerate(distances[:stage]):
            if held >> k & 1:
                quarter = flip(quarter, other)
        slot = held + 2 ** stage
        return pltpu.make_async_remote_copy(
            src_ref=lent_rows(i, quarter),
            dst_ref=lent_rows(i, quarter),
            send_sem=share_send.at[i, slot],
            recv_sem=lend_recv.at[i, slot],
            device_id={"panel": flip(panel, distance)},
            device_id_type=MESH,
        )

    def lend_out(i):
        pl.when(z == 0)(lambda: lend(i).start())

    def pass_around(i, stage):
        @pl.when(z == 1)
        def _():
            if stage == 0:
                lend(i).wait_recv()
            else:
                for held in range(2 ** (stage - 1)):
                    pass_on(i, stage - 1, held).wait_recv()
            for held in range(2 ** stage):
                pass_on(i, stage, held).start()

    def lent_here(i):
        for held in range(2 ** (len(distances) - 1)):
            pass_on(i, len(distances) - 1, held).wait_recv()
        helping[i] = jnp.zeros((rows, columns), jnp.float32)

    def lent_left(i):
        @pl.when(z == 1)
        def _():
            for stage in range(len(distances)):
                for held in range(2 ** stage):
                    pass_on(i, stage, held).wait_send()
            hand(i).wait_send()

        pl.when(z == 0)(lambda: lend(i).wait_send())

    def hand(i):
        return pltpu.make_async_remote_copy(
            src_ref=part.at[i],
            dst_ref=part.at[i],
            send_sem=part_send.at[i],
            recv_sem=part_recv.at[i],
            device_id={"leaf": below},
            device_id_type=MESH,
        )

    def finish(front):
        if front in HELPED:
            i = HELPED.index(front)

            @pl.when(z == 0)
            def _():
                hand(i).wait_recv()
                acc[front % 4] += part[i].astype(jnp.float32)

        solved = live(front) * acc[front % 4]
        out[front] = solved
        if front < 3:
            gather = 7 + front
            rows_of(gather, leaf, 0, 1)[...] = solved.astype(jnp.bfloat16).reshape(piece_units, unit, columns)
            publish(gather, True)
        tall = min(rows, 128)
        for i in range(rows // tall):
            strip = solved[i * tall:(i + 1) * tall]
            sums[panel, pl.ds(front, 1), i * tall:(i + 1) * tall] = jnp.sum(
                (strip * strip).T, axis=0, keepdims=True
            )

    def solve(fronts, orders):
        for front in fronts:
            acc[front % 4] = jnp.zeros((rows, columns), jnp.float32)

        @pl.loop(1, depth - z + 1)
        def _(step):
            layer = z + step

            for front in fronts:
                more = layer < depth
                if front in HELPED:
                    more = more & (z > 0)
                pl.when(more)(lambda: relay(front, layer, DOWN))
                pl.when(step == 1)(lambda: cross(front, False))

            done = layer - 1
            start = pl.multiple_of(done * pair, pair)
            def gain(front, order):
                for chunk in range(chunks_of(front) // 2):
                    arrived(front, done, 1 - y, chunk)

                @pl.when(done > z)
                def _():
                    for chunk in range(chunks_of(front) // 2, chunks_of(front)):
                        arrived(front, done, 1 - y, chunk)

                pl.when(step == 1)(lambda: load(order).wait())
                acc[front % 4] += jnp.dot(
                    mats[order % SLOTS, :, pl.ds(start, pair)],
                    red[front, pl.ds(start, pair), :],
                    preferred_element_type=jnp.float32,
                )

            def help_below(front):
                i = HELPED.index(front)
                pl.when(step == 1)(lambda: lent_here(i))
                helping[i] += jnp.dot(
                    lent[i, :, pl.ds(pl.multiple_of(start - pair, pair), pair)],
                    red[front, pl.ds(start, pair), :],
                    preferred_element_type=jnp.float32,
                )

                @pl.when(layer == depth)
                def _():
                    part[i] = helping[i].astype(jnp.bfloat16)
                    hand(i).start()

            for front, order in zip(fronts, orders):
                if front in HELPED:
                    pl.when((z > 0) | (done == 0))(lambda: gain(front, order))
                    pl.when(z == 1)(lambda: help_below(front))
                else:
                    gain(front, order)
                pl.when(layer == depth)(lambda: finish(front))

        for order in orders:
            release(order)

    def share(fronts):
        @pl.loop(z + 1, depth)
        def _(layer):
            for front in fronts:
                relay(7 + front, layer, DOWN)

        for front in fronts:
            cross(7 + front, True)

        @pl.loop(1, z + 1)
        def _(step):
            for front in fronts:
                relay(7 + front, z - step, UP)

    def share_end(front):
        @pl.loop(0, depth)
        def _(layer):
            for chunk in range(chunks_of(7 + front) // 2):
                arrived(7 + front, layer, 1 - y, chunk)

            @pl.when(layer != z)
            def _():
                for chunk in range(chunks_of(7 + front) // 2, chunks_of(7 + front)):
                    arrived(7 + front, layer, 1 - y, chunk)

    stages = len(distances)
    lend_out(0)
    publish_reduced(0, None)
    solve([0], [0])
    share([0])
    share_end(0)
    lend_out(1)
    pass_around(0, 0)
    couple(1, 1, root)
    couple(2, 2, root)
    anc0[0:units] = root[...]
    anc1[0:units] = root[...]
    solve([1, 2], [3, 4])
    for stage in range(1, stages):
        pass_around(0, stage)
    pass_around(1, 0)
    share([1, 2])
    share_end(1)
    couple(3, 5, anc0)
    couple(4, 6, anc0)
    share_end(2)
    for stage in range(1, stages):
        pass_around(1, stage)
    couple(5, 7, anc1)
    couple(6, 8, anc1)
    solve([3, 4, 5, 6], [9, 10, 11, 12])

    def exchange(hop):
        return pltpu.make_async_remote_copy(
            src_ref=sums.at[panel],
            dst_ref=sums.at[panel],
            send_sem=sums_send.at[hop],
            recv_sem=sums_recv.at[hop],
            device_id={"panel": lax.rem(panel + hop, panels)},
            device_id_type=MESH,
        )

    for hop in range(1, panels):
        exchange(hop).start()

    def left(gather, layer, chunk, way, allowed=None):
        if allowed is None:
            transfer(gather, layer, y, chunk, way).wait_send()
        else:
            pl.when(allowed)(lambda: transfer(gather, layer, y, chunk, way).wait_send())

    @pl.loop(0, depth)
    def _(layer):
        near = (layer == z - 1) | (layer == z + 1)
        for gather in range(10):
            for chunk in range(chunks_of(gather)):
                sideways = layer >= 0 if gather >= 7 else layer >= z
                if gather in HELPED:
                    sideways = sideways & ((z > 0) | (layer == 0))
                if chunk >= chunks_of(gather) // 2:
                    sideways = sideways & jnp.logical_not(near)
                left(gather, layer, chunk, SIDE, sideways)
                left(gather, layer, chunk, DOWN, sinks(gather) & (layer >= z))
                if gather >= 7:
                    left(gather, layer, chunk, UP, has_up & (layer <= z))

    for gather in range(10):
        for chunk in range(chunks_of(gather) // 2, chunks_of(gather)):
            pl.when(sinks(gather))(lambda: transfer(gather, z, 1 - y, chunk, DOWN, True).wait_send())
            if gather >= 7:
                pl.when(has_up)(lambda: transfer(gather, z, 1 - y, chunk, UP, True).wait_send())

    for i in range(len(HELPED)):
        lent_left(i)

    for hop in range(1, panels):
        exchange(hop).wait()
    total = sums[0]
    for i in range(1, panels):
        total = total + sums[i]
    power[...] = total[0:7] / jnp.float32(total_columns)


def local(leaves, panels, right_sides, inverse_diagonal, off_diagonal, structure, pivot_counts):
    fronts, rows, columns = right_sides.shape
    pivots = inverse_diagonal.shape[2]
    coupled = off_diagonal.shape[2]
    unit = math.gcd(rows // share_chunks(rows), coupled // structure.shape[1])
    bf16, f32 = jnp.bfloat16, jnp.float32
    vmem = pl.BlockSpec(memory_space=pltpu.VMEM)
    smem = pl.BlockSpec(memory_space=pltpu.SMEM)
    anywhere = pl.BlockSpec(memory_space=pl.ANY)
    return pl.pallas_call(
        functools.partial(kernel, leaves, panels, columns * panels),
        out_shape=(
            jax.ShapeDtypeStruct((fronts, rows, columns), f32),
            jax.ShapeDtypeStruct((fronts, rows), f32),
        ),
        in_specs=[vmem, anywhere, anywhere, smem, smem],
        out_specs=(vmem, vmem),
        scratch_shapes=[
            pltpu.VMEM((7, pivots, columns), bf16),
            pltpu.VMEM((pivots // unit, unit, columns), bf16),
            pltpu.VMEM((2 * pivots // unit, unit, columns), bf16),
            pltpu.VMEM((2 * pivots // unit, unit, columns), bf16),
            pltpu.VMEM((SLOTS, rows, max(pivots, coupled)), bf16),
            pltpu.VMEM((coupled, columns), bf16),
            pltpu.VMEM((4, rows, columns), f32),
            pltpu.VMEM((panels, 8, rows), f32),
            pltpu.VMEM((len(HELPED), rows, pivots - 2 * rows), bf16),
            pltpu.VMEM((len(HELPED), rows, columns), f32),
            pltpu.VMEM((len(HELPED), rows, columns), bf16),
            pltpu.SemaphoreType.DMA((SLOTS,)),
            pltpu.SemaphoreType.DMA((10, 3, share_chunks(rows) * leaves // 2)),
            pltpu.SemaphoreType.DMA((10, 2, share_chunks(rows))),
            pltpu.SemaphoreType.DMA((10, share_chunks(rows) * leaves)),
            pltpu.SemaphoreType.DMA((panels,)),
            pltpu.SemaphoreType.DMA((panels,)),
            pltpu.SemaphoreType.DMA((len(HELPED),)),
            pltpu.SemaphoreType.DMA((len(HELPED), panels)),
            pltpu.SemaphoreType.DMA((len(HELPED), panels)),
            pltpu.SemaphoreType.DMA((len(HELPED),)),
            pltpu.SemaphoreType.DMA((len(HELPED),)),
        ],
        compiler_params=pltpu.CompilerParams(
            collective_id=0, has_side_effects=True, vmem_limit_bytes=60 * 2**20
        ),
        cost_estimate=pl.CostEstimate(
            flops=13 * 2 * rows * pivots * columns,
            bytes_accessed=13 * 2 * rows * pivots,
            transcendentals=0,
        ),
    )(right_sides, inverse_diagonal, off_diagonal, structure, pivot_counts)


def solution(mesh):
    placed = (P(None, "leaf", "panel"), P(None, "leaf", None), P(None, "leaf", None), P(), P())
    return jax.shard_map(
        functools.partial(local, mesh.shape["leaf"], mesh.shape["panel"]),
        mesh=mesh,
        in_specs=placed,
        out_specs=(P(None, "leaf", "panel"), P(None, "leaf")),
        check_vma=False,
    )
```

```python
import functools
import math

import jax
import jax.numpy as jnp
from jax import lax
from jax.experimental import pallas as pl
from jax.experimental.pallas import tpu as pltpu
from jax.sharding import PartitionSpec as P

SLOTS = 7
HELPED = (3, 4)
DOWN, UP, SIDE = 0, 1, 2
MESH = pl.DeviceIdType.MESH


def share_chunks(rows):
    return min(2, rows // 16)


def kernel(
    leaves, panels, total_columns,
    given, inv, off, structure, counts,
    samples, power,
    rhs, out, red, root, anc0, anc1, mats, picked, acc, sums, lent, helping, part,
    given_sem, out_sem, mat_sem, send_sem, cross_sem, recv_sem, sums_send, sums_recv,
    lend_send, lend_recv, share_send, part_send, part_recv,
):
    leaf = lax.axis_index("leaf")
    panel = lax.axis_index("panel")
    depth = leaves // 2
    z, y = leaf // 2, leaf % 2
    rows, columns = rhs.shape[1], rhs.shape[2]
    pivots = red.shape[1]
    coupled = off.shape[2]
    listed = structure.shape[1]
    block = coupled // listed
    pair = 2 * rows
    wide = min(coupled, 1024)
    unit = root.shape[1]

    def chunks_of(gather):
        return 2 if gather < 7 else share_chunks(rows)

    units, piece_units = pivots // unit, rows // unit

    sequence = [(inv, 0), (off, 0), (off, 1), (inv, 1), (inv, 2)]
    sequence += [(off, 2 + i) for i in range(4)] + [(inv, 3 + i) for i in range(4)]

    def load(i):
        source, which = sequence[i]
        slot = i % SLOTS
        return pltpu.make_async_copy(source.at[which], mats.at[slot], mat_sem.at[slot])

    def release(i):
        if i + SLOTS < len(sequence):
            load(i + SLOTS).start()

    def take_in(front):
        return pltpu.make_async_copy(given.at[front], rhs.at[front], given_sem.at[front])

    def put_out(front):
        return pltpu.make_async_copy(out.at[front], samples.at[front], out_sem.at[front])

    take_in(0).start()
    for i in range(min(SLOTS, len(sequence))):
        load(i).start()
    for front in range(1, 7):
        take_in(front).start()

    has_down, has_up = z > 0, z < depth - 1

    barrier = pltpu.get_barrier_semaphore()

    def greet(target):
        pl.semaphore_signal(barrier, inc=1, device_id=target, device_id_type=MESH)

    below, above, beside = leaf - 2, leaf + 2, leaf + 1 - 2 * y
    pl.when(has_down)(lambda: greet({"leaf": below}))
    pl.when(has_up)(lambda: greet({"leaf": above}))
    greet({"leaf": beside})
    for hop in range(1, panels):
        greet({"panel": lax.rem(panel + hop, panels)})
    pl.semaphore_wait(barrier, panels + has_down.astype(jnp.int32) + has_up.astype(jnp.int32))

    def rows_of(gather, piece, chunk, chunks):
        index = piece * chunks + chunk
        if gather < 7:
            size = rows // chunks
            return red.at[gather, pl.ds(pl.multiple_of(index * size, size), size)]
        size = piece_units // chunks
        if gather == 7:
            return root.at[pl.ds(index * size, size)]
        return (anc0, anc1)[gather - 8].at[pl.ds(units + index * size, size)]

    def transfer(gather, layer, side, chunk, way, cross=False):
        piece = 2 * layer + side
        chunks = chunks_of(gather)
        held = rows_of(gather, piece, chunk, chunks)
        place = layer * chunks + chunk
        return pltpu.make_async_remote_copy(
            src_ref=held,
            dst_ref=held,
            send_sem=cross_sem.at[gather, way, chunk] if cross else send_sem.at[gather, way, place],
            recv_sem=recv_sem.at[gather, piece * chunks + chunk],
            device_id={"leaf": (below, above, beside)[way]},
            device_id_type=MESH,
        )

    def send(gather, layer, chunk, way):
        transfer(gather, layer, y, chunk, way).start()

    def arrived(gather, layer, side, chunk):
        transfer(gather, layer, side, chunk, SIDE).wait_recv()

    def sinks(gather):
        return z > 1 if gather in HELPED else has_down

    def relay(gather, layer, way):
        for chunk in range(chunks_of(gather)):
            arrived(gather, layer, y, chunk)
            pl.when(has_up if way == UP else sinks(gather))(lambda: send(gather, layer, chunk, way))
            if chunk < chunks_of(gather) // 2:
                send(gather, layer, chunk, SIDE)
            else:
                near = (layer == z - 1) | (layer == z + 1)
                pl.when(jnp.logical_not(near))(lambda: send(gather, layer, chunk, SIDE))

    def cross(gather, upward):
        for chunk in range(chunks_of(gather) // 2, chunks_of(gather)):
            arrived(gather, z, 1 - y, chunk)
            if upward:
                pl.when(has_up)(lambda: transfer(gather, z, 1 - y, chunk, UP, True).start())
            pl.when(sinks(gather))(lambda: transfer(gather, z, 1 - y, chunk, DOWN, True).start())

    def publish(gather, upward):
        for chunk in range(chunks_of(gather)):
            if upward:
                pl.when(has_up)(lambda: send(gather, z, chunk, UP))
            pl.when(sinks(gather))(lambda: send(gather, z, chunk, DOWN))
            send(gather, z, chunk, SIDE)

    position = leaf * rows + lax.broadcasted_iota(jnp.int32, (rows, columns), 0)

    def live(front):
        return jnp.clip(counts[front] - position, 0, 1).astype(jnp.float32)

    def publish_reduced(front, update):
        take_in(front).wait()
        value = rhs[front] if update is None else rhs[front] - update
        rows_of(front, leaf, 0, 1)[...] = (live(front) * value).astype(jnp.bfloat16)
        publish(front, False)

    def couple(front, order, ancestors):
        parts = block // unit
        for i in range(listed):
            number = structure[front - 1, i]
            if ancestors is anc1:
                per_front = pivots // block
                number = jnp.minimum(number, jnp.maximum(number - per_front, per_front - 1))
            for j in range(parts):
                picked[pl.ds(i * block + j * unit, unit), :] = ancestors[number * parts + j]
        load(order).wait()
        acc[0] = jnp.zeros((rows, columns), jnp.float32)

        @pl.loop(0, coupled // wide)
        def _(i):
            start = pl.multiple_of(i * wide, wide)
            acc[0] += jnp.dot(
                mats[order % SLOTS, :, pl.ds(start, wide)],
                picked[pl.ds(start, wide), :],
                preferred_element_type=jnp.float32,
            )

        release(order)
        publish_reduced(front, acc[0])

    share_rows = rows // panels

    def lent_rows(i, quarter):
        return lent.at[i, pl.ds(pl.multiple_of(quarter * share_rows, share_rows), share_rows)]

    def lend(i):
        taken = pl.ds(pl.multiple_of(panel * share_rows, share_rows), share_rows)
        return pltpu.make_async_remote_copy(
            src_ref=inv.at[HELPED[i], taken, pl.ds(pair, pivots - pair)],
            dst_ref=lent_rows(i, panel),
            send_sem=lend_send.at[i],
            recv_sem=lend_recv.at[i, 0],
            device_id={"leaf": above},
            device_id_type=MESH,
        )

    def flip(at, distance):
        return at + distance - 2 * distance * ((at // distance) % 2)

    distances = []
    while 2 ** len(distances) < panels:
        distances.append(panels // 2 ** (len(distances) + 1))

    def pass_on(i, stage, held):
        distance = distances[stage]
        quarter = panel
        for k, other in enumerate(distances[:stage]):
            if held >> k & 1:
                quarter = flip(quarter, other)
        slot = held + 2 ** stage
        return pltpu.make_async_remote_copy(
            src_ref=lent_rows(i, quarter),
            dst_ref=lent_rows(i, quarter),
            send_sem=share_send.at[i, slot],
            recv_sem=lend_recv.at[i, slot],
            device_id={"panel": flip(panel, distance)},
            device_id_type=MESH,
        )

    def lend_out(i):
        pl.when(z == 0)(lambda: lend(i).start())

    def pass_around(i, stage):
        @pl.when(z == 1)
        def _():
            if stage == 0:
                lend(i).wait_recv()
            else:
                for held in range(2 ** (stage - 1)):
                    pass_on(i, stage - 1, held).wait_recv()
            for held in range(2 ** stage):
                pass_on(i, stage, held).start()

    def lent_here(i):
        for held in range(2 ** (len(distances) - 1)):
            pass_on(i, len(distances) - 1, held).wait_recv()
        helping[i] = jnp.zeros((rows, columns), jnp.float32)

    def lent_left(i):
        @pl.when(z == 1)
        def _():
            for stage in range(len(distances)):
                for held in range(2 ** stage):
                    pass_on(i, stage, held).wait_send()
            hand(i).wait_send()

        pl.when(z == 0)(lambda: lend(i).wait_send())

    def hand(i):
        return pltpu.make_async_remote_copy(
            src_ref=part.at[i],
            dst_ref=part.at[i],
            send_sem=part_send.at[i],
            recv_sem=part_recv.at[i],
            device_id={"leaf": below},
            device_id_type=MESH,
        )

    def finish(front):
        if front in HELPED:
            i = HELPED.index(front)

            @pl.when(z == 0)
            def _():
                hand(i).wait_recv()
                acc[front % 4] += part[i].astype(jnp.float32)

        solved = live(front) * acc[front % 4]
        if front < 3:
            gather = 7 + front
            rows_of(gather, leaf, 0, 1)[...] = solved.astype(jnp.bfloat16).reshape(piece_units, unit, columns)
            publish(gather, True)
        out[front] = solved
        put_out(front).start()
        tall = min(rows, 128)
        for i in range(rows // tall):
            strip = solved[i * tall:(i + 1) * tall]
            sums[panel, pl.ds(front, 1), i * tall:(i + 1) * tall] = jnp.sum(
                (strip * strip).T, axis=0, keepdims=True
            )

    def solve(fronts, orders):
        for front in fronts:
            acc[front % 4] = jnp.zeros((rows, columns), jnp.float32)

        @pl.loop(1, depth - z + 1)
        def _(step):
            layer = z + step

            for front in fronts:
                more = layer < depth
                if front in HELPED:
                    more = more & (z > 0)
                pl.when(more)(lambda: relay(front, layer, DOWN))
                pl.when(step == 1)(lambda: cross(front, False))

            done = layer - 1
            start = pl.multiple_of(done * pair, pair)
            def gain(front, order):
                for chunk in range(chunks_of(front) // 2):
                    arrived(front, done, 1 - y, chunk)

                @pl.when(done > z)
                def _():
                    for chunk in range(chunks_of(front) // 2, chunks_of(front)):
                        arrived(front, done, 1 - y, chunk)

                pl.when(step == 1)(lambda: load(order).wait())
                acc[front % 4] += jnp.dot(
                    mats[order % SLOTS, :, pl.ds(start, pair)],
                    red[front, pl.ds(start, pair), :],
                    preferred_element_type=jnp.float32,
                )

            def help_below(front):
                i = HELPED.index(front)
                pl.when(step == 1)(lambda: lent_here(i))
                helping[i] += jnp.dot(
                    lent[i, :, pl.ds(pl.multiple_of(start - pair, pair), pair)],
                    red[front, pl.ds(start, pair), :],
                    preferred_element_type=jnp.float32,
                )

                @pl.when(layer == depth)
                def _():
                    part[i] = helping[i].astype(jnp.bfloat16)
                    hand(i).start()

            for front, order in zip(fronts, orders):
                if front in HELPED:
                    pl.when((z > 0) | (done == 0))(lambda: gain(front, order))
                    pl.when(z == 1)(lambda: help_below(front))
                else:
                    gain(front, order)
                pl.when(layer == depth)(lambda: finish(front))

        for order in orders:
            release(order)

    def share(fronts):
        @pl.loop(z + 1, depth)
        def _(layer):
            for front in fronts:
                relay(7 + front, layer, DOWN)

        for front in fronts:
            cross(7 + front, True)

        @pl.loop(1, z + 1)
        def _(step):
            for front in fronts:
                relay(7 + front, z - step, UP)

    def share_end(front):
        @pl.loop(0, depth)
        def _(layer):
            for chunk in range(chunks_of(7 + front) // 2):
                arrived(7 + front, layer, 1 - y, chunk)

            @pl.when(layer != z)
            def _():
                for chunk in range(chunks_of(7 + front) // 2, chunks_of(7 + front)):
                    arrived(7 + front, layer, 1 - y, chunk)

    stages = len(distances)
    lend_out(0)
    publish_reduced(0, None)
    solve([0], [0])
    share([0])
    share_end(0)
    lend_out(1)
    pass_around(0, 0)
    couple(1, 1, root)
    couple(2, 2, root)
    anc0[0:units] = root[...]
    anc1[0:units] = root[...]
    solve([1, 2], [3, 4])
    for stage in range(1, stages):
        pass_around(0, stage)
    pass_around(1, 0)
    share([1, 2])
    share_end(1)
    couple(3, 5, anc0)
    couple(4, 6, anc0)
    share_end(2)
    for stage in range(1, stages):
        pass_around(1, stage)
    couple(5, 7, anc1)
    couple(6, 8, anc1)
    solve([3, 4, 5, 6], [9, 10, 11, 12])

    def exchange(hop):
        return pltpu.make_async_remote_copy(
            src_ref=sums.at[panel],
            dst_ref=sums.at[panel],
            send_sem=sums_send.at[hop],
            recv_sem=sums_recv.at[hop],
            device_id={"panel": lax.rem(panel + hop, panels)},
            device_id_type=MESH,
        )

    for hop in range(1, panels):
        exchange(hop).start()

    def left(gather, layer, chunk, way, allowed=None):
        if allowed is None:
            transfer(gather, layer, y, chunk, way).wait_send()
        else:
            pl.when(allowed)(lambda: transfer(gather, layer, y, chunk, way).wait_send())

    @pl.loop(0, depth)
    def _(layer):
        near = (layer == z - 1) | (layer == z + 1)
        for gather in range(10):
            for chunk in range(chunks_of(gather)):
                sideways = layer >= 0 if gather >= 7 else layer >= z
                if gather in HELPED:
                    sideways = sideways & ((z > 0) | (layer == 0))
                if chunk >= chunks_of(gather) // 2:
                    sideways = sideways & jnp.logical_not(near)
                left(gather, layer, chunk, SIDE, sideways)
                left(gather, layer, chunk, DOWN, sinks(gather) & (layer >= z))
                if gather >= 7:
                    left(gather, layer, chunk, UP, has_up & (layer <= z))

    for gather in range(10):
        for chunk in range(chunks_of(gather) // 2, chunks_of(gather)):
            pl.when(sinks(gather))(lambda: transfer(gather, z, 1 - y, chunk, DOWN, True).wait_send())
            if gather >= 7:
                pl.when(has_up)(lambda: transfer(gather, z, 1 - y, chunk, UP, True).wait_send())

    for i in range(len(HELPED)):
        lent_left(i)

    for hop in range(1, panels):
        exchange(hop).wait()
    for front in range(7):
        put_out(front).wait()
    total = sums[0]
    for i in range(1, panels):
        total = total + sums[i]
    power[...] = total[0:7] / jnp.float32(total_columns)


def local(leaves, panels, right_sides, inverse_diagonal, off_diagonal, structure, pivot_counts):
    fronts, rows, columns = right_sides.shape
    pivots = inverse_diagonal.shape[2]
    coupled = off_diagonal.shape[2]
    unit = math.gcd(rows // share_chunks(rows), coupled // structure.shape[1])
    bf16, f32 = jnp.bfloat16, jnp.float32
    vmem = pl.BlockSpec(memory_space=pltpu.VMEM)
    smem = pl.BlockSpec(memory_space=pltpu.SMEM)
    anywhere = pl.BlockSpec(memory_space=pl.ANY)
    return pl.pallas_call(
        functools.partial(kernel, leaves, panels, columns * panels),
        out_shape=(
            jax.ShapeDtypeStruct((fronts, rows, columns), f32),
            jax.ShapeDtypeStruct((fronts, rows), f32),
        ),
        in_specs=[anywhere, anywhere, anywhere, smem, smem],
        out_specs=(anywhere, vmem),
        scratch_shapes=[
            pltpu.VMEM((fronts, rows, columns), f32),
            pltpu.VMEM((fronts, rows, columns), f32),
            pltpu.VMEM((7, pivots, columns), bf16),
            pltpu.VMEM((pivots // unit, unit, columns), bf16),
            pltpu.VMEM((2 * pivots // unit, unit, columns), bf16),
            pltpu.VMEM((2 * pivots // unit, unit, columns), bf16),
            pltpu.VMEM((SLOTS, rows, max(pivots, coupled)), bf16),
            pltpu.VMEM((coupled, columns), bf16),
            pltpu.VMEM((4, rows, columns), f32),
            pltpu.VMEM((panels, 8, rows), f32),
            pltpu.VMEM((len(HELPED), rows, pivots - 2 * rows), bf16),
            pltpu.VMEM((len(HELPED), rows, columns), f32),
            pltpu.VMEM((len(HELPED), rows, columns), bf16),
            pltpu.SemaphoreType.DMA((fronts,)),
            pltpu.SemaphoreType.DMA((fronts,)),
            pltpu.SemaphoreType.DMA((SLOTS,)),
            pltpu.SemaphoreType.DMA((10, 3, share_chunks(rows) * leaves // 2)),
            pltpu.SemaphoreType.DMA((10, 2, share_chunks(rows))),
            pltpu.SemaphoreType.DMA((10, share_chunks(rows) * leaves)),
            pltpu.SemaphoreType.DMA((panels,)),
            pltpu.SemaphoreType.DMA((panels,)),
            pltpu.SemaphoreType.DMA((len(HELPED),)),
            pltpu.SemaphoreType.DMA((len(HELPED), panels)),
            pltpu.SemaphoreType.DMA((len(HELPED), panels)),
            pltpu.SemaphoreType.DMA((len(HELPED),)),
            pltpu.SemaphoreType.DMA((len(HELPED),)),
        ],
        compiler_params=pltpu.CompilerParams(
            collective_id=0, has_side_effects=True, vmem_limit_bytes=60 * 2**20
        ),
        cost_estimate=pl.CostEstimate(
            flops=13 * 2 * rows * pivots * columns,
            bytes_accessed=13 * 2 * rows * pivots,
            transcendentals=0,
        ),
    )(right_sides, inverse_diagonal, off_diagonal, structure, pivot_counts)


def solution(mesh):
    placed = (P(None, "leaf", "panel"), P(None, "leaf", None), P(None, "leaf", None), P(), P())
    return jax.shard_map(
        functools.partial(local, mesh.shape["leaf"], mesh.shape["panel"]),
        mesh=mesh,
        in_specs=placed,
        out_specs=(P(None, "leaf", "panel"), P(None, "leaf")),
        check_vma=False,
    )
```
